128 devices in a mesh: inp: 16 (over y, z), tgt: 4 (over x_hi, core), mdl: 2 (over x_lo).
Axes of the slice: x: 4 (x_hi: 2, x_lo: 2; x = x_hi * 2 + x_lo), y: 4, z: 4, core: 2. Of those that a mesh axis runs over, the one named last changes fastest.
Arguments:
- encoder: bfloat16 [8192, 4096], P('inp'), may hold values from -8 to 8
- key_weight: bfloat16 [2, 4096, 2, 4, 256], P(None, None, 'mdl', 'tgt'), may hold values from -1 to 1
- value_weight: bfloat16 [2, 4096, 2, 4, 256], P(None, None, 'mdl', 'tgt'), may hold values from -0.09375 to 0.09375
- queries: bfloat16 [2, 2048, 8, 256], P(None, 'tgt', 'mdl'), may hold values from -8 to 8
- grad_out: bfloat16 [2, 2048, 8, 256], P(None, 'tgt', 'mdl'), may hold values from -6 to 6
Outputs:
- grad_query: bfloat16 [2, 2048, 8, 256], P(None, 'tgt', 'mdl')
- grad_encoder: bfloat16 [8192, 4096], P('inp', ('tgt', 'mdl'))
The draws below stay inside these ranges and needn't reach their ends.
All inputs are finite; a program needn't handle non-finite values.
Results may differ from the reference program's by a relative error of at most 0.019.
The reference program's roundings to bfloat16 on the way count: a program that leaves them out, or rounds other values in their place, can miss the bound.
Values may be sent and summed in bfloat16 or wider, within the bound.
A program may use at most 128 MiB of HBM per device.

```python
import math
import jax
import jax.numpy as jnp
from jax import lax

D = 4096
HEADS = 8
HS = 256
LAYERS = 2
ENC = 8192
DEC = 2048
HPG = 4
N_MDL = 2


def encoder_row(source, row_index):
    row_key = jax.random.fold_in(jax.random.fold_in(source, 101), row_index)
    row_values = jnp.clip(jax.random.normal(row_key, (D,), jnp.float32), -6.0, 6.0)
    rising = 0.8 + 0.5 * row_index.astype(jnp.float32) / ENC
    return row_values * rising


def key_weight_flat(source):
    weight_key = jax.random.fold_in(source, 102)
    raw_values = jax.random.normal(weight_key, (LAYERS, D, HEADS, HS), jnp.float32)
    return jnp.clip(raw_values, -4.0, 4.0) / math.sqrt(D)


def draw_encoder(key, part):
    positions = jnp.arange(ENC, dtype=jnp.int32)
    values = jax.vmap(lambda row_index: encoder_row(key, row_index))(positions)
    return values.astype(jnp.bfloat16)


def draw_key_weight(key, part):
    values = key_weight_flat(key).reshape(LAYERS, D, HEADS // HPG, HPG, HS)
    return values.astype(jnp.bfloat16)


def draw_queries(key, part):
    key = jax.random.fold_in(key, 3)
    values = jnp.clip(jax.random.normal(key, (LAYERS, DEC, HEADS, HS), jnp.float32), -6.0, 6.0) * 0.12
    return values.astype(jnp.bfloat16)


def block_levels(rng, extent, pieces, least, top_value):
    def one(position, blocks):
        draws = jax.random.uniform(jax.random.fold_in(jax.random.fold_in(rng, 6), position), (blocks,), jnp.float32, least / len(pieces), top_value / len(pieces))
        return jnp.repeat(jnp.exp(draws), extent[position] // blocks).reshape((-1,) + (1,) * (len(extent) - position - 1))

    loudness = one(*pieces[0])
    for cut in pieces[1:]:
        loudness = loudness * one(*cut)
    return loudness


def bell_draw(key, dims, deviation, limit, cuts=(), kind=jnp.bfloat16):
    values = deviation * jax.random.normal(key, dims, jnp.float32)
    if cuts:
        values = values * block_levels(key, dims, cuts, -0.22, 0.18)
    return jnp.clip(values, -limit, limit).astype(kind)


def setup_inputs(seed: int = 0) -> dict:
    streams_of = jax.random.split(jax.random.key(seed), 6)
    encoder = draw_encoder(jax.random.fold_in(streams_of[5], 71), 0)
    key_weight = draw_key_weight(jax.random.fold_in(streams_of[5], 71), 0)
    value_weight = bell_draw(streams_of[2], (LAYERS, D, N_MDL, HPG, HS), D ** -0.5, 0.09375, ((2, 2), (3, 4)))
    queries = draw_queries(jax.random.fold_in(streams_of[5], 71), 0)
    grad_out = bell_draw(streams_of[4], (LAYERS, DEC, HEADS, HS), 1.0, 6.0, ((1, 4), (2, 2)))
    return {"encoder": encoder, "key_weight": key_weight, "value_weight": value_weight, "queries": queries, "grad_out": grad_out}


def head_grads(operands):
    query_head, grad_head, key_head, value_head = operands
    scores = jnp.dot(query_head, key_head.T, preferred_element_type=jnp.float32)
    shifted = jnp.exp(scores - jnp.max(scores, axis=1, keepdims=True))
    attention = shifted / jnp.sum(shifted, axis=1, keepdims=True)
    dprobs = jnp.dot(grad_head, value_head.T, preferred_element_type=jnp.float32)
    row_inner = jnp.sum(attention * dprobs, axis=1, keepdims=True)
    dscores = (attention * (dprobs - row_inner)).astype(jnp.bfloat16)
    attention_low = attention.astype(jnp.bfloat16)
    query_grad = jnp.dot(dscores, key_head, preferred_element_type=jnp.float32).astype(jnp.bfloat16)
    key_grad = jnp.dot(dscores.T, query_head, preferred_element_type=jnp.float32).astype(jnp.bfloat16)
    value_grad = jnp.dot(attention_low.T, grad_head, preferred_element_type=jnp.float32).astype(jnp.bfloat16)
    return query_grad, key_grad, value_grad


def reference(encoder, key_weight, value_weight, queries, grad_out):
    grad_layers = []
    enc_grad = jnp.zeros((ENC, D), jnp.float32)
    for layer_index in range(LAYERS):
        key_matrix = key_weight[layer_index].reshape(D, HEADS * HS)
        value_matrix = value_weight[layer_index].reshape(D, HEADS * HS)
        key_block = jnp.dot(encoder, key_matrix, preferred_element_type=jnp.float32).astype(jnp.bfloat16).reshape(ENC, HEADS, HS)
        value_block = jnp.dot(encoder, value_matrix, preferred_element_type=jnp.float32).astype(jnp.bfloat16).reshape(ENC, HEADS, HS)
        operands = (jnp.swapaxes(queries[layer_index], 0, 1), jnp.swapaxes(grad_out[layer_index], 0, 1),
                    jnp.swapaxes(key_block, 0, 1), jnp.swapaxes(value_block, 0, 1))
        query_grad, key_grad, value_grad = lax.map(head_grads, operands)
        grad_layers.append(jnp.swapaxes(query_grad, 0, 1))
        key_flat = jnp.swapaxes(key_grad, 0, 1).reshape(ENC, HEADS * HS)
        value_flat = jnp.swapaxes(value_grad, 0, 1).reshape(ENC, HEADS * HS)
        enc_grad = enc_grad + jnp.dot(key_flat, key_matrix.T, preferred_element_type=jnp.float32)
        enc_grad = enc_grad + jnp.dot(value_flat, value_matrix.T, preferred_element_type=jnp.float32)
    return jnp.stack(grad_layers), enc_grad.astype(jnp.bfloat16)
```

```python
import functools

import jax
import jax.numpy as jnp
from jax import lax
from jax.experimental import pallas as pl
from jax.experimental.pallas import tpu as pltpu
from jax.sharding import PartitionSpec as P

MESH = pl.DeviceIdType.MESH
F32 = jnp.float32
BF16 = jnp.bfloat16
NT = (((1,), (1,)), ((), ()))

E = 512
D = 4096
C = 256
L = 2
N = 2048
CH = 8
NSEM = 128


def kernel(
    enc_hbm, kw_hbm, vw_hbm, q_hbm, g_hbm,
    dq_out, enc_out,
    enc, w, qg, kv, kt, pbuf, dpbuf, dsb, alb,
    stat_s, stat_r, stat_f,
    dqs, r1, s1, r2, dqt,
    grads, eb, cr, rl, nb,
    send_sems, recv_sems, local_sems,
):
    inp = lax.axis_index("inp")
    tgt = lax.axis_index("tgt")
    mdl = lax.axis_index("mdl")
    y, z = inp // 4, inp % 4
    xh, core = tgt // 2, tgt % 2
    x = xh * 2 + mdl

    def at_yz(yy, zz):
        return (yy * 4 + zz, tgt, mdl)

    def at_x(xx, cc):
        return (inp, (xx // 2) * 2 + cc, xx % 2)

    counter = [0]
    sent = []

    def put(src, dst, device):
        k = counter[0]
        counter[0] += 1
        cp = pltpu.make_async_remote_copy(
            src_ref=src, dst_ref=dst, send_sem=send_sems.at[k], recv_sem=recv_sems.at[k],
            device_id=device, device_id_type=MESH,
        )
        cp.start()
        sent.append(cp)
        return cp

    local_counter = [0]

    def load(src, dst):
        k = local_counter[0]
        local_counter[0] += 1
        cp = pltpu.make_async_copy(src, dst, local_sems.at[k])
        cp.start()
        return cp

    barrier = pltpu.get_barrier_semaphore()

    @pl.loop(1, 16)
    def _(o):
        pl.semaphore_signal(barrier, inc=1, device_id=((inp + o) % 16, tgt, mdl), device_id_type=MESH)

    @pl.loop(1, 8)
    def _(o):
        r = (tgt * 2 + mdl + o) % 8
        pl.semaphore_signal(barrier, inc=1, device_id=(inp, r // 2, r % 2), device_id_type=MESH)

    enc_load = load(enc_hbm, enc)
    own_q = load(q_hbm.at[tgt], qg.at[:, 0, :, :, tgt])
    own_g = load(g_hbm.at[tgt], qg.at[:, 1, :, :, tgt])
    w_loads = []
    for l in range(L):
        w_loads.append(load(kw_hbm.at[l], w.at[2 * l]))
        w_loads.append(load(vw_hbm.at[l], w.at[2 * l + 1]))

    stat_s[...] = jnp.zeros_like(stat_s)
    pl.semaphore_wait(barrier, 22)

    partner_t = xh * 2 + (1 - core)
    opp = (1 - xh) * 2
    x_phase, core_phase = [], []
    for r in range(2):
        there = opp + (core + r) % 2
        for k, src in enumerate((q_hbm, g_hbm)):
            x_phase.append(put(src.at[there, :, y, z], qg.at[:, k, y, z, tgt], (inp, there, mdl)))
    for k, src in enumerate((q_hbm, g_hbm)):
        core_phase.append(put(src.at[partner_t], qg.at[:, k, :, :, tgt], (inp, partner_t, mdl)))

    def plane_device(half, phase, d):
        if (half == 0) == (phase == 0):
            return at_yz((y + d) % 4, z)
        return at_yz(y, (z + d) % 4)

    def gather_phase(view, phase):
        out = []
        for d in range(1, 4):
            for half in range(2):
                if phase == 0:
                    ref = view(half, y, z)
                elif half == 0:
                    ref = view(half, slice(None), z)
                else:
                    ref = view(half, y, slice(None))
                out.append(put(ref, ref, plane_device(half, phase, d)))
        return out

    def arrive(cps):
        for cp in cps:
            cp.wait_recv()

    def qview(l):
        return lambda half, yy, zz: qg.at[l, half, yy, zz, pl.ds(opp, 2)]

    def project(j):
        w_loads[j].wait()
        val = jnp.dot(enc[...], w[j], preferred_element_type=F32).astype(BF16)
        kv[j] = val

    enc_load.wait()
    project(0)
    arrive(x_phase)
    q_a0 = gather_phase(qview(0), 0)
    project(1)
    q_a1 = gather_phase(qview(1), 0)
    arrive(q_a0)
    q_b0 = gather_phase(qview(0), 1)
    project(2)
    arrive(q_a1)
    q_b1 = gather_phase(qview(1), 1)
    project(3)
    for l in range(L):
        kt[l] = kv[2 * l].astype(F32).T.astype(BF16)
    own_q.wait()
    own_g.wait()
    arrive(core_phase)

    def scores(l, lo, hi):
        @pl.loop(lo, hi)
        def _(n):
            yy, zz = n // 2, (n % 2) * 2
            qc = qg[l, 0, yy, pl.ds(zz, 2)].reshape(256, C)
            gc = qg[l, 1, yy, pl.ds(zz, 2)].reshape(256, C)
            st = lax.dot_general(kv[2 * l], qc, NT, preferred_element_type=F32)
            dp = lax.dot_general(kv[2 * l + 1], gc, NT, preferred_element_type=F32)
            peak = jnp.max(st, axis=0, keepdims=True)
            p = jnp.exp(st - peak)
            pbuf[l, n] = p
            dpbuf[l, n] = dp
            total = jnp.sum(p, axis=0, keepdims=True)
            inner = jnp.sum(p * dp, axis=0, keepdims=True)
            for k in range(2):
                cols = slice(128 * k, 128 * k + 128)
                stat_s[l, 2 * n + k, 0:1, :] = peak[:, cols]
                stat_s[l, 2 * n + k, 1:2, :] = total[:, cols]
                stat_s[l, 2 * n + k, 2:3, :] = inner[:, cols]

    stat_sems = {}

    def stats_out(l, phase):
        k = counter[0]
        counter[0] += 1
        stat_sems[l, phase] = k

        @pl.loop(1, 16)
        def _(o):
            there = (inp + o) % 16
            if phase == 0:
                src, dst = stat_s.at[l, there], stat_r.at[l, o - 1]
            else:
                src, dst = stat_f.at[l, inp], stat_f.at[l, inp]
            pltpu.make_async_remote_copy(
                src_ref=src, dst_ref=dst, send_sem=send_sems.at[k], recv_sem=recv_sems.at[k],
                device_id=(there, tgt, mdl), device_id_type=MESH,
            ).start()

    def stats_in(l, phase, sems):
        k = stat_sems[l, phase]
        pltpu.make_async_copy(stat_r.at[l], stat_r.at[l], sems.at[k]).wait()

    def combine(l):
        stats_in(l, 0, recv_sems)
        own = stat_s[l, inp]
        got = stat_r[l]
        peaks = got[:, 0, :]
        peak = jnp.maximum(jnp.max(peaks, axis=0, keepdims=True), own[0:1])
        f = jnp.exp(peaks - peak)
        fo = jnp.exp(own[0:1] - peak)
        total = jnp.sum(got[:, 1, :] * f, axis=0, keepdims=True) + own[1:2] * fo
        inner = jnp.sum(got[:, 2, :] * f, axis=0, keepdims=True) + own[2:3] * fo
        stat_f[l, inp] = jnp.concatenate(
            [peak, total, inner / total, jnp.zeros((5, 128), F32)], axis=0
        )
        stats_out(l, 1)

    arrive(q_b0)
    scores(0, 0, CH)
    stats_out(0, 0)
    arrive(q_b1)
    scores(1, 0, CH // 2)
    combine(0)
    scores(1, CH // 2, CH)
    stats_out(1, 0)

    def dscores(l):
        stats_in(l, 1, recv_sems)

        @pl.loop(0, CH)
        def _(n):
            def row(ref, r):
                return jnp.concatenate([ref[l, 2 * n, r : r + 1], ref[l, 2 * n + 1, r : r + 1]], axis=1)

            fac = jnp.exp(row(stat_s, 0) - row(stat_f, 0)) / row(stat_f, 1)
            inner = row(stat_f, 2)
            a = pbuf[l, n] * fac
            ds = (a * (dpbuf[l, n] - inner)).astype(BF16)
            cols = pl.ds(pl.multiple_of(n * 256, 256), 256)
            dsb[:, cols] = ds
            alb[:, cols] = a.astype(BF16)
            dqc = jnp.dot(kt[l], ds, preferred_element_type=F32).astype(BF16)
            yy, zz = n // 2, (n % 2) * 2
            for half in range(2):
                for k in range(2):
                    dqs[l, half, yy, zz + k] = dqc[128 * half : 128 * half + 128, 128 * k : 128 * k + 128]

    def kv_grads(l):
        qf = qg[l, 0].reshape(N, C)
        gf = qg[l, 1].reshape(N, C)
        grads[2 * l] = jnp.dot(dsb[...], qf, preferred_element_type=F32).astype(BF16)
        grads[2 * l + 1] = jnp.dot(alb[...], gf, preferred_element_type=F32).astype(BF16)

    def rs_first(l):
        out = []
        for d in range(1, 4):
            out.append(put(dqs.at[l, 0, (y + d) % 4], r1.at[l, 0, d - 1], plane_device(0, 0, d)))
            out.append(put(dqs.at[l, 1, :, (z + d) % 4], r1.at[l, 1, d - 1], plane_device(1, 0, d)))
        return out

    def rs_second(l, first):
        arrive(first)
        for half in range(2):
            own = dqs[l, 0, y] if half == 0 else dqs[l, 1, :, z]
            acc = own.astype(F32)
            for d in range(3):
                acc = acc + r1[l, half, d].astype(F32)
            s1[l, half] = acc.astype(BF16)
        out = []
        for d in range(1, 4):
            out.append(put(s1.at[l, 0, (z + d) % 4], r2.at[l, 0, d - 1], plane_device(0, 1, d)))
            out.append(put(s1.at[l, 1, (y + d) % 4], r2.at[l, 1, d - 1], plane_device(1, 1, d)))
        return out

    def rs_end(l, second):
        arrive(second)
        for half in range(2):
            acc = (s1[l, 0, z] if half == 0 else s1[l, 1, y]).astype(F32)
            for d in range(3):
                acc = acc + r2[l, half, d].astype(F32)
            dqt[l, :, :, 128 * half : 128 * half + 128] = acc.T.reshape(4, 32, 128).astype(BF16)
        out = [
            put(dqt.at[l, (tgt + d) % 4], dq_out.at[l, tgt, y, z], (inp, (tgt + d) % 4, mdl))
            for d in range(1, 4)
        ]
        mine = load(dqt.at[l, tgt], dq_out.at[l, tgt, y, z])
        return out, mine

    def oview(l):
        return lambda half, yy, zz: dq_out.at[l, pl.ds(2 * half, 2), yy, zz]

    dscores(0)
    f0 = rs_first(0)
    combine(1)
    kv_grads(0)
    e0 = rs_second(0, f0)
    dscores(1)
    f1 = rs_first(1)
    x0, m0 = rs_end(0, e0)
    kv_grads(1)

    def block(xx, cc):
        f = (xx // 2) * 4 + cc * 2 + xx % 2
        rows = pl.ds(pl.multiple_of(f * 512, 512), 512)
        acc = lax.dot_general(grads[0], w[0, rows, :], NT, preferred_element_type=F32)
        for j in range(1, 4):
            acc = acc + lax.dot_general(grads[j], w[j, rows, :], NT, preferred_element_type=F32)
        return acc.astype(BF16)

    def both(k, xx):
        eb[k, 0] = block(xx, 1 - core)
        cp = put(eb.at[k, 0], cr.at[k], at_x(x, 1 - core))
        eb[k, 1] = block(xx, core)
        return cp

    xp, xm, xo = (x + 1) % 4, (x + 3) % 4, (x + 2) % 4

    arrive(x0)
    m0.wait()
    a0 = gather_phase(oview(0), 0)
    c_o = both(0, xo)
    e1 = rs_second(1, f1)
    arrive([c_o])
    eb[0, 1] = eb[0, 1] + cr[0]
    ro = [
        put(eb.at[0, 1, pl.ds(0, 256)], rl.at[0], at_x(xp, core)),
        put(eb.at[0, 1, pl.ds(256, 256)], rl.at[1], at_x(xm, core)),
    ]
    arrive(a0)
    b0 = gather_phase(oview(0), 1)
    c_p = both(1, xp)
    c_m = both(2, xm)
    arrive([c_p, c_m])
    eb[1, 1] = eb[1, 1] + cr[1]
    eb[2, 1] = eb[2, 1] + cr[2]
    n1 = [
        put(eb.at[1, 1, pl.ds(256, 256)], nb.at[0, pl.ds(256, 256)], at_x(xp, core)),
        put(eb.at[2, 1, pl.ds(0, 256)], nb.at[1, pl.ds(0, 256)], at_x(xm, core)),
    ]
    x1, m1 = rs_end(1, e1)
    arrive(ro)
    eb[1, 1, 0:256] = eb[1, 1, 0:256] + rl[0]
    eb[2, 1, 256:512] = eb[2, 1, 256:512] + rl[1]
    n2 = [
        put(eb.at[1, 1, pl.ds(0, 256)], nb.at[0, pl.ds(0, 256)], at_x(xp, core)),
        put(eb.at[2, 1, pl.ds(256, 256)], nb.at[1, pl.ds(256, 256)], at_x(xm, core)),
    ]
    c_s = both(3, x)
    arrive(x1)
    m1.wait()
    a1 = gather_phase(oview(1), 0)
    arrive([c_s])
    arrive(a1)
    b1 = gather_phase(oview(1), 1)
    arrive(n1)
    arrive(n2)
    enc_out[...] = (
        eb[3, 1].astype(F32) + cr[3].astype(F32) + nb[0].astype(F32) + nb[1].astype(F32)
    ).astype(BF16)
    arrive(b0)
    arrive(b1)
    for cp in sent:
        cp.wait_send()
    for (l, phase) in stat_sems:
        stats_in(l, phase, send_sems)


def body(encoder, key_weight, value_weight, queries, grad_out):
    kw = key_weight.reshape(L, D, C)
    vw = value_weight.reshape(L, D, C)
    q = jnp.transpose(queries, (2, 0, 1, 3)).reshape(4, L, 4, 4, 32, C)
    g = jnp.transpose(grad_out, (2, 0, 1, 3)).reshape(4, L, 4, 4, 32, C)
    anywhere = pl.BlockSpec(memory_space=pl.ANY)
    dq, de = pl.pallas_call(
        kernel,
        out_shape=(
            jax.ShapeDtypeStruct((L, 4, 4, 4, 32, C), BF16),
            jax.ShapeDtypeStruct((E, 512), BF16),
        ),
        in_specs=[anywhere] * 5,
        out_specs=(anywhere, pl.BlockSpec(memory_space=pltpu.VMEM)),
        scratch_shapes=[
            pltpu.VMEM((E, D), BF16),
            pltpu.VMEM((4, D, C), BF16),
            pltpu.VMEM((L, 2, 4, 4, 4, 32, C), BF16),
            pltpu.VMEM((4, E, C), BF16),
            pltpu.VMEM((L, C, E), BF16),
            pltpu.VMEM((L, CH, E, 256), F32),
            pltpu.VMEM((L, CH, E, 256), F32),
            pltpu.VMEM((E, N), BF16),
            pltpu.VMEM((E, N), BF16),
            pltpu.VMEM((L, 16, 8, 128), F32),
            pltpu.VMEM((L, 15, 8, 128), F32),
            pltpu.VMEM((L, 16, 8, 128), F32),
            pltpu.VMEM((L, 2, 4, 4, 128, 128), BF16),
            pltpu.VMEM((L, 2, 3, 4, 128, 128), BF16),
            pltpu.VMEM((L, 2, 4, 128, 128), BF16),
            pltpu.VMEM((L, 2, 3, 128, 128), BF16),
            pltpu.VMEM((L, 4, 32, C), BF16),
            pltpu.VMEM((4, E, C), BF16),
            pltpu.VMEM((4, 2, E, 512), BF16),
            pltpu.VMEM((4, E, 512), BF16),
            pltpu.VMEM((2, 256, 512), BF16),
            pltpu.VMEM((2, E, 512), BF16),
            pltpu.SemaphoreType.DMA((NSEM,)),
            pltpu.SemaphoreType.DMA((NSEM,)),
            pltpu.SemaphoreType.DMA((16,)),
        ],
        compiler_params=pltpu.CompilerParams(
            collective_id=0, has_side_effects=True, vmem_limit_bytes=60 * 2**20
        ),
        cost_estimate=pl.CostEstimate(flops=14_000_000_000, bytes_accessed=20_000_000, transcendentals=2_000_000),
    )(encoder, kw, vw, q, g)
    dq = jnp.transpose(dq.reshape(L, 4, 512, C), (0, 2, 1, 3))
    return dq, de


def solution(mesh):
    placed = (
        P("inp", None),
        P(None, None, "mdl", "tgt", None),
        P(None, None, "mdl", "tgt", None),
        P(None, "tgt", "mdl", None),
        P(None, "tgt", "mdl", None),
    )
    return jax.shard_map(
        body,
        mesh=mesh,
        in_specs=placed,
        out_specs=(P(None, "tgt", "mdl", None), P("inp", ("tgt", "mdl"))),
        check_vma=False,
    )
```

```python
import functools

import jax
import jax.numpy as jnp
from jax import lax
from jax.experimental import pallas as pl
from jax.experimental.pallas import tpu as pltpu
from jax.sharding import PartitionSpec as P

MESH = pl.DeviceIdType.MESH
F32 = jnp.float32
BF16 = jnp.bfloat16
NT = (((1,), (1,)), ((), ()))

E = 512
D = 4096
C = 256
L = 2
N = 2048
NSEM = 128


def kernel(
    enc_hbm, kw_hbm, vw_hbm, q_hbm, g_hbm,
    dq_out, enc_out,
    enc, w, qg, kv, kt, pbuf, dpbuf, dsb, alb,
    stat_s, stat_r, stat_c, fac, inn,
    dqs, r1, s1, r2, dqt, ob,
    kvacc, grads, eb, cr, rl, nb,
    send_sems, recv_sems, local_sems,
):
    inp = lax.axis_index("inp")
    tgt = lax.axis_index("tgt")
    mdl = lax.axis_index("mdl")
    y, z = inp // 4, inp % 4
    xh, core = tgt // 2, tgt % 2
    x = xh * 2 + mdl
    opp = (1 - xh) * 2
    partner = xh * 2 + (1 - core)
    xp, xm, xo = (x + 1) % 4, (x + 3) % 4, (x + 2) % 4

    def at_yz(yy, zz):
        return (yy * 4 + zz, tgt, mdl)

    def at_x(xx, cc):
        return (inp, (xx // 2) * 2 + cc, xx % 2)

    counter = [0]
    sent = []

    def put(src, dst, device):
        k = counter[0]
        counter[0] += 1
        cp = pltpu.make_async_remote_copy(
            src_ref=src, dst_ref=dst, send_sem=send_sems.at[k], recv_sem=recv_sems.at[k],
            device_id=device, device_id_type=MESH,
        )
        cp.start()
        sent.append(cp)
        return cp

    local_counter = [0]

    def load(src, dst):
        k = local_counter[0]
        local_counter[0] += 1
        cp = pltpu.make_async_copy(src, dst, local_sems.at[k])
        cp.start()
        return cp

    def arrive(cps):
        for cp in cps:
            cp.wait_recv()

    barrier = pltpu.get_barrier_semaphore()
    friends = [at_yz((y + d) % 4, z) for d in range(1, 4)] + [at_yz(y, (z + d) % 4) for d in range(1, 4)]
    friends += [(inp, partner, mdl), (inp, opp, mdl), (inp, opp + 1, mdl), at_x(xp, core), at_x(xm, core)]
    for friend in friends:
        pl.semaphore_signal(barrier, inc=1, device_id=friend, device_id_type=MESH)

    enc_load = load(enc_hbm, enc)
    w_loads = []
    for l in range(L):
        w_loads.append(
            (load(kw_hbm.at[l], w.at[l, :, pl.ds(0, C)]), load(vw_hbm.at[l], w.at[l, :, pl.ds(C, C)]))
        )
        if l == 0:
            own = [load(src.at[tgt], qg.at[:, k, 0, :, :, core]) for k, src in enumerate((q_hbm, g_hbm))]

    def plane_device(half, phase, d):
        if (half == 0) == (phase == 0):
            return at_yz((y + d) % 4, z)
        return at_yz(y, (z + d) % 4)

    def gather_phase(view, phase):
        out = []
        for d in range(1, 4):
            for half in range(2):
                if phase == 0:
                    ref = view(half, y, z)
                elif half == 0:
                    ref = view(half, slice(None), z)
                else:
                    ref = view(half, y, slice(None))
                out.append(put(ref, ref, plane_device(half, phase, d)))
        return out

    def qview(l):
        if l == 0:
            return lambda half, yy, zz: qg.at[0, half, 1, yy, zz]
        return lambda half, yy, zz: qg.at[1, 0, 1, yy, zz, half]

    def project(l):
        for cp in w_loads[l]:
            cp.wait()
        kv[l] = jnp.dot(enc[...], w[l], preferred_element_type=F32).astype(BF16)
        kt[l] = kv[l, :, 0:C].astype(F32).T.astype(BF16)

    def scores(grp, l):
        @pl.loop(0, 4)
        def _(n):
            qc = qg[l, 0, grp, n].reshape(256, C)
            gc = qg[l, 1, grp, n].reshape(256, C)
            st = lax.dot_general(kv[l, :, 0:C], qc, NT, preferred_element_type=F32)
            dp = lax.dot_general(kv[l, :, C : 2 * C], gc, NT, preferred_element_type=F32)
            peak = jnp.max(st, axis=0, keepdims=True)
            p = jnp.exp(st - peak)
            pbuf[grp, l, n] = p
            dpbuf[grp, l, n] = dp
            total = jnp.sum(p, axis=0, keepdims=True)
            inner = jnp.sum(p * dp, axis=0, keepdims=True)
            for k in range(2):
                cols = slice(128 * k, 128 * k + 128)
                row = pl.ds(l * 8 + 2 * n + k, 1)
                stat_s[grp, 0, row, :] = peak[:, cols]
                stat_s[grp, 1, row, :] = total[:, cols]
                stat_s[grp, 2, row, :] = inner[:, cols]

    def stats_out(grp, phase):
        src = (stat_s if phase == 0 else stat_c).at[grp]
        return [put(src, stat_r.at[grp, phase, d - 1], plane_device(0, phase, d)) for d in range(1, 4)]

    def stats_in(grp, phase, cps):
        arrive(cps)
        src = stat_s if phase == 0 else stat_c
        terms = [(src[grp, 0], src[grp, 1], src[grp, 2])]
        for d in range(3):
            terms.append((stat_r[grp, phase, d, 0], stat_r[grp, phase, d, 1], stat_r[grp, phase, d, 2]))
        peak = jnp.maximum(jnp.maximum(terms[0][0], terms[1][0]), jnp.maximum(terms[2][0], terms[3][0]))
        scale = [jnp.exp(t[0] - peak) for t in terms]
        total = sum(t[1] * f for t, f in zip(terms, scale))
        inner = sum(t[2] * f for t, f in zip(terms, scale))
        if phase == 0:
            stat_c[grp, 0] = peak
            stat_c[grp, 1] = total
            stat_c[grp, 2] = inner
        else:
            fac[grp] = jnp.exp(stat_s[grp, 0] - peak) / total
            inn[grp] = inner / total

    low = lax.broadcasted_iota(jnp.int32, (C, 128), 1) < 64

    def dscores(grp):
        @pl.loop(0, 4)
        def _(n):
            dqc = []
            for l in range(L):
                def row(ref):
                    return jnp.concatenate([ref[grp, pl.ds(l * 8 + 2 * n + k, 1), :] for k in range(2)], axis=1)

                a = pbuf[grp, l, n] * row(fac)
                ds = (a * (dpbuf[grp, l, n] - row(inn))).astype(BF16)
                cols = pl.ds(pl.multiple_of(n * 256, 256), 256)
                dsb[l, :, cols] = ds
                alb[l, :, cols] = a.astype(BF16)
                dqc.append(jnp.dot(kt[l], ds, preferred_element_type=F32))
            for k in range(2):
                one, two = (v[:, 128 * k : 128 * k + 128] for v in dqc)
                even = jnp.where(low, one, pltpu.roll(two, 64, 1)).astype(BF16)
                odd = jnp.where(low, pltpu.roll(one, 64, 1), two).astype(BF16)
                for half in range(2):
                    rows = slice(128 * half, 128 * half + 128)
                    dqs[grp, half, n, 2 * k] = even[rows]
                    dqs[grp, half, n, 2 * k + 1] = odd[rows]

    def kv_grads(grp):
        for l in range(L):
            for k, left in enumerate((dsb, alb)):
                val = jnp.dot(left[l], qg[l, k, grp].reshape(N // 2, C), preferred_element_type=F32)
                if grp == 0:
                    kvacc[l, k] = val
                else:
                    grads[l, :, k * C : k * C + C] = (kvacc[l, k] + val).astype(BF16)

    def rs_first(grp):
        out = []
        for d in range(1, 4):
            out.append(put(dqs.at[grp, 0, (y + d) % 4], r1.at[grp, 0, d - 1], plane_device(0, 0, d)))
            out.append(put(dqs.at[grp, 1, :, (z + d) % 4], r1.at[grp, 1, d - 1], plane_device(1, 0, d)))
        return out

    def rs_second(grp, first):
        arrive(first)
        for half in range(2):
            own_part = dqs[grp, 0, y] if half == 0 else dqs[grp, 1, :, z]
            acc = own_part.astype(F32)
            for d in range(3):
                acc = acc + r1[grp, half, d].astype(F32)
            s1[grp, half] = acc.astype(BF16)
        out = []
        for d in range(1, 4):
            out.append(put(s1.at[grp, 0, (z + d) % 4], r2.at[grp, 0, d - 1], plane_device(0, 1, d)))
            out.append(put(s1.at[grp, 1, (y + d) % 4], r2.at[grp, 1, d - 1], plane_device(1, 1, d)))
        return out

    def rs_end(grp, second):
        arrive(second)
        for half in range(2):
            acc = (s1[grp, 0, z] if half == 0 else s1[grp, 1, y]).astype(F32)
            for d in range(3):
                acc = acc + r2[grp, half, d].astype(F32)
            dqt[grp, :, :, :, 128 * half : 128 * half + 128] = acc.T.reshape(2, 2, 32, 128).astype(BF16)
        if grp == 0:
            mine = load(dqt.at[0, :, core], ob.at[:, tgt, y, z])
            out = [put(dqt.at[0, :, 1 - core], ob.at[:, tgt, y, z], (inp, partner, mdl))]
            return out, mine
        out = []
        for r in range(2):
            c = (core + r) % 2
            out.append(put(dqt.at[1, :, c], ob.at[:, tgt, y, z], (inp, opp + c, mdl)))
        return out, None

    def oview(grp):
        first = xh * 2 if grp == 0 else opp
        return lambda half, yy, zz: ob.at[half, pl.ds(first, 2), yy, zz]

    def store(grp):
        first = xh * 2 if grp == 0 else opp
        return load(ob.at[:, pl.ds(first, 2)], dq_out.at[:, pl.ds(first, 2)])

    def block(xx, cc):
        f = (xx // 2) * 4 + cc * 2 + xx % 2
        rows = pl.ds(pl.multiple_of(f * 512, 512), 512)
        acc = lax.dot_general(grads[0], w[0, rows, :], NT, preferred_element_type=F32)
        acc = acc + lax.dot_general(grads[1], w[1, rows, :], NT, preferred_element_type=F32)
        return acc.astype(BF16)

    def both(k, xx):
        eb[k, 0] = block(xx, 1 - core)
        cp = put(eb.at[k, 0], cr.at[k], at_x(x, 1 - core))
        eb[k, 1] = block(xx, core)
        return cp

    pl.semaphore_wait(barrier, len(friends))

    x_phase, x_whole, core_phase = [], [], []
    for r in range(2):
        there = opp + (core + r) % 2
        device = (inp, there, mdl)
        x_phase.append(put(g_hbm.at[there, 0, y, z], qg.at[0, 1, 1, y, z, core], device))
        x_phase.append(put(q_hbm.at[there, :, y, z], qg.at[:, 0, 1, y, z, core], device))
    for k, src in enumerate((q_hbm, g_hbm)):
        core_phase.append(put(src.at[partner], qg.at[:, k, 0, :, :, core], (inp, partner, mdl)))
    for r in range(2):
        there = opp + (core + r) % 2
        x_whole.append(put(g_hbm.at[there, 1], qg.at[1, 1, 1, :, :, core], (inp, there, mdl)))

    enc_load.wait()
    project(0)
    project(1)
    for cp in own:
        cp.wait()
    arrive(core_phase)
    scores(0, 0)
    scores(0, 1)
    sa = stats_out(0, 0)
    arrive(x_phase)
    q_a0 = gather_phase(qview(0), 0)
    q_a1 = gather_phase(qview(1), 0)
    stats_in(0, 0, sa)
    sa = stats_out(0, 1)
    arrive(q_a0)
    q_b0 = gather_phase(qview(0), 1)
    arrive(q_a1)
    q_b1 = gather_phase(qview(1), 1)
    stats_in(0, 1, sa)
    dscores(0)
    fa = rs_first(0)
    kv_grads(0)
    arrive(q_b0)
    scores(1, 0)
    arrive(q_b1)
    arrive(x_whole)
    scores(1, 1)
    sb = stats_out(1, 0)
    ea = rs_second(0, fa)
    stats_in(1, 0, sb)
    sb = stats_out(1, 1)
    xa, ma = rs_end(0, ea)
    stats_in(1, 1, sb)
    dscores(1)
    fb = rs_first(1)
    arrive(xa)
    ma.wait()
    aa = gather_phase(oview(0), 0)
    kv_grads(1)
    c_o = both(0, xo)
    c_p = both(1, xp)
    arrive([c_o])
    eb[0, 1] = eb[0, 1] + cr[0]
    ro = [
        put(eb.at[0, 1, pl.ds(0, 256)], rl.at[0], at_x(xp, core)),
        put(eb.at[0, 1, pl.ds(256, 256)], rl.at[1], at_x(xm, core)),
    ]
    c_m = both(2, xm)
    arrive(aa)
    ba = gather_phase(oview(0), 1)
    arrive([c_p, c_m])
    eb[1, 1] = eb[1, 1] + cr[1]
    eb[2, 1] = eb[2, 1] + cr[2]
    n1 = [
        put(eb.at[1, 1, pl.ds(256, 256)], nb.at[0, pl.ds(256, 256)], at_x(xp, core)),
        put(eb.at[2, 1, pl.ds(0, 256)], nb.at[1, pl.ds(0, 256)], at_x(xm, core)),
    ]
    e2 = rs_second(1, fb)
    c_s = both(3, x)
    arrive(ro)
    eb[1, 1, 0:256] = eb[1, 1, 0:256] + rl[0]
    eb[2, 1, 256:512] = eb[2, 1, 256:512] + rl[1]
    n2 = [
        put(eb.at[1, 1, pl.ds(0, 256)], nb.at[0, pl.ds(0, 256)], at_x(xp, core)),
        put(eb.at[2, 1, pl.ds(256, 256)], nb.at[1, pl.ds(256, 256)], at_x(xm, core)),
    ]
    xb, _ = rs_end(1, e2)
    arrive(xb)
    ab = gather_phase(oview(1), 0)
    arrive([c_s])
    arrive(ba)
    out_a = store(0)
    arrive(ab)
    bb = gather_phase(oview(1), 1)
    arrive(n1)
    arrive(n2)
    enc_out[...] = (
        eb[3, 1].astype(F32) + cr[3].astype(F32) + nb[0].astype(F32) + nb[1].astype(F32)
    ).astype(BF16)
    arrive(bb)
    out_b = store(1)
    for cp in sent:
        cp.wait_send()
    out_a.wait()
    out_b.wait()


def body(encoder, key_weight, value_weight, queries, grad_out):
    kw = key_weight.reshape(L, D, C)
    vw = value_weight.reshape(L, D, C)
    q = jnp.transpose(queries, (2, 0, 1, 3)).reshape(4, L, 4, 4, 32, C)
    g = jnp.transpose(grad_out, (2, 0, 1, 3)).reshape(4, L, 4, 4, 32, C)
    anywhere = pl.BlockSpec(memory_space=pl.ANY)
    dq, de = pl.pallas_call(
        kernel,
        out_shape=(
            jax.ShapeDtypeStruct((L, 4, 4, 4, 32, C), BF16),
            jax.ShapeDtypeStruct((E, 512), BF16),
        ),
        in_specs=[anywhere] * 5,
        out_specs=(anywhere, pl.BlockSpec(memory_space=pltpu.VMEM)),
        scratch_shapes=[
            pltpu.VMEM((E, D), BF16),
            pltpu.VMEM((L, D, 2 * C), BF16),
            pltpu.VMEM((L, 2, 2, 4, 4, 2, 32, C), BF16),
            pltpu.VMEM((L, E, 2 * C), BF16),
            pltpu.VMEM((L, C, E), BF16),
            pltpu.VMEM((2, L, 4, E, 256), F32),
            pltpu.VMEM((2, L, 4, E, 256), F32),
            pltpu.VMEM((L, E, N // 2), BF16),
            pltpu.VMEM((L, E, N // 2), BF16),
            pltpu.VMEM((2, 3, 16, 128), F32),
            pltpu.VMEM((2, 2, 3, 3, 16, 128), F32),
            pltpu.VMEM((2, 3, 16, 128), F32),
            pltpu.VMEM((2, 16, 128), F32),
            pltpu.VMEM((2, 16, 128), F32),
            pltpu.VMEM((2, 2, 4, 4, 128, 128), BF16),
            pltpu.VMEM((2, 2, 3, 4, 128, 128), BF16),
            pltpu.VMEM((2, 2, 4, 128, 128), BF16),
            pltpu.VMEM((2, 2, 3, 128, 128), BF16),
            pltpu.VMEM((2, L, 2, 32, C), BF16),
            pltpu.VMEM((L, 4, 4, 4, 32, C), BF16),
            pltpu.VMEM((L, 2, E, C), F32),
            pltpu.VMEM((L, E, 2 * C), BF16),
            pltpu.VMEM((4, 2, E, 512), BF16),
            pltpu.VMEM((4, E, 512), BF16),
            pltpu.VMEM((2, 256, 512), BF16),
            pltpu.VMEM((2, E, 512), BF16),
            pltpu.SemaphoreType.DMA((NSEM,)),
            pltpu.SemaphoreType.DMA((NSEM,)),
            pltpu.SemaphoreType.DMA((16,)),
        ],
        compiler_params=pltpu.CompilerParams(
            collective_id=0, has_side_effects=True, vmem_limit_bytes=60 * 2**20
        ),
        cost_estimate=pl.CostEstimate(flops=14_000_000_000, bytes_accessed=20_000_000, transcendentals=2_000_000),
    )(encoder, kw, vw, q, g)
    dq = jnp.transpose(dq.reshape(L, 4, 512, C), (0, 2, 1, 3))
    return dq, de


def solution(mesh):
    placed = (
        P("inp", None),
        P(None, None, "mdl", "tgt", None),
        P(None, None, "mdl", "tgt", None),
        P(None, "tgt", "mdl", None),
        P(None, "tgt", "mdl", None),
    )
    return jax.shard_map(
        body,
        mesh=mesh,
        in_specs=placed,
        out_specs=(P(None, "tgt", "mdl", None), P("inp", ("tgt", "mdl"))),
        check_vma=False,
    )
```

```python
import functools

import jax
import jax.numpy as jnp
from jax import lax
from jax.experimental import pallas as pl
from jax.experimental.pallas import tpu as pltpu
from jax.sharding import PartitionSpec as P

MESH = pl.DeviceIdType.MESH
F32 = jnp.float32
BF16 = jnp.bfloat16
NT = (((1,), (1,)), ((), ()))

E = 512
D = 4096
C = 256
L = 2
N = 2048
NSEM = 108


def kernel(
    enc_hbm, kw_hbm, vw_hbm, q_hbm, g_hbm,
    dq_out, enc_out,
    enc, w, qg, kv, kt, pbuf, dpbuf, dsb, alb,
    stat_s, stat_r, stat_c, fac, inn,
    dqs, r1, s1, r2, dqt, ob,
    kvacc, grads, eb, cr, rl, nb,
    send_sems, recv_sems, local_sems,
):
    inp = lax.axis_index("inp")
    tgt = lax.axis_index("tgt")
    mdl = lax.axis_index("mdl")
    y, z = inp // 4, inp % 4
    xh, core = tgt // 2, tgt % 2
    x = xh * 2 + mdl
    opp = (1 - xh) * 2
    partner = xh * 2 + (1 - core)
    xp, xm, xo = (x + 1) % 4, (x + 3) % 4, (x + 2) % 4

    def at_yz(yy, zz):
        return (yy * 4 + zz, tgt, mdl)

    def at_x(xx, cc):
        return (inp, (xx // 2) * 2 + cc, xx % 2)

    counter = [0]
    sent = []

    def put(src, dst, device):
        k = counter[0]
        counter[0] += 1
        cp = pltpu.make_async_remote_copy(
            src_ref=src, dst_ref=dst, send_sem=send_sems.at[k], recv_sem=recv_sems.at[k],
            device_id=device, device_id_type=MESH,
        )
        cp.start()
        sent.append(cp)
        return cp

    local_counter = [0]

    def load(src, dst):
        k = local_counter[0]
        local_counter[0] += 1
        cp = pltpu.make_async_copy(src, dst, local_sems.at[k])
        cp.start()
        return cp

    def arrive(cps):
        for cp in cps:
            cp.wait_recv()

    barrier = pltpu.get_barrier_semaphore()
    friends = [at_yz((y + d) % 4, z) for d in range(1, 4)] + [at_yz(y, (z + d) % 4) for d in range(1, 4)]
    friends += [(inp, partner, mdl), (inp, opp, mdl), (inp, opp + 1, mdl), at_x(xp, core), at_x(xm, core)]
    for friend in friends:
        pl.semaphore_signal(barrier, inc=1, device_id=friend, device_id_type=MESH)

    enc_load = load(enc_hbm, enc)
    w_loads = []
    for l in range(L):
        w_loads.append(
            (load(kw_hbm.at[l], w.at[l, :, pl.ds(0, C)]), load(vw_hbm.at[l], w.at[l, :, pl.ds(C, C)]))
        )
        if l == 0:
            own = [load(src.at[tgt], qg.at[:, k, 0, :, :, core]) for k, src in enumerate((q_hbm, g_hbm))]

    def plane_device(half, phase, d):
        if (half == 0) == (phase == 0):
            return at_yz((y + d) % 4, z)
        return at_yz(y, (z + d) % 4)

    def gather_phase(view, phase, to=None):
        to = to or view
        out = []
        for d in range(1, 4):
            for half in range(2):
                if phase == 0:
                    place = (half, y, z)
                elif half == 0:
                    place = (half, slice(None), z)
                else:
                    place = (half, y, slice(None))
                out.append(put(view(*place), to(*place), plane_device(half, phase, d)))
        return out

    def qview(l):
        if l == 0:
            return lambda half, yy, zz: qg.at[0, half, 1, yy, zz]
        return lambda half, yy, zz: qg.at[1, 0, 1, yy, zz, half]

    def project(l):
        for cp in w_loads[l]:
            cp.wait()
        kv[l] = jnp.dot(enc[...], w[l], preferred_element_type=F32).astype(BF16)
        kt[l] = kv[l, :, 0:C].astype(F32).T.astype(BF16)

    def scores(grp, l):
        @pl.loop(0, 4)
        def _(n):
            qc = qg[l, 0, grp, n].reshape(256, C)
            gc = qg[l, 1, grp, n].reshape(256, C)
            st = lax.dot_general(kv[l, :, 0:C], qc, NT, preferred_element_type=F32)
            dp = lax.dot_general(kv[l, :, C : 2 * C], gc, NT, preferred_element_type=F32)
            peak = jnp.max(st, axis=0, keepdims=True)
            p = jnp.exp(st - peak)
            pbuf[grp, l, n] = p
            dpbuf[grp, l, n] = dp
            total = jnp.sum(p, axis=0, keepdims=True)
            inner = jnp.sum(p * dp, axis=0, keepdims=True)
            for k in range(2):
                cols = slice(128 * k, 128 * k + 128)
                row = pl.ds(l * 8 + 2 * n + k, 1)
                stat_s[grp, 0, row, :] = peak[:, cols]
                stat_s[grp, 1, row, :] = total[:, cols]
                stat_s[grp, 2, row, :] = inner[:, cols]

    def stats_out(grp, phase):
        src = (stat_s if phase == 0 else stat_c).at[grp]
        return [put(src, stat_r.at[grp, phase, d - 1], plane_device(0, phase, d)) for d in range(1, 4)]

    def stats_in(grp, phase, cps):
        arrive(cps)
        src = stat_s if phase == 0 else stat_c
        terms = [(src[grp, 0], src[grp, 1], src[grp, 2])]
        for d in range(3):
            terms.append((stat_r[grp, phase, d, 0], stat_r[grp, phase, d, 1], stat_r[grp, phase, d, 2]))
        peak = jnp.maximum(jnp.maximum(terms[0][0], terms[1][0]), jnp.maximum(terms[2][0], terms[3][0]))
        scale = [jnp.exp(t[0] - peak) for t in terms]
        total = sum(t[1] * f for t, f in zip(terms, scale))
        inner = sum(t[2] * f for t, f in zip(terms, scale))
        if phase == 0:
            stat_c[grp, 0] = peak
            stat_c[grp, 1] = total
            stat_c[grp, 2] = inner
        else:
            fac[grp] = jnp.exp(stat_s[grp, 0] - peak) / total
            inn[grp] = inner / total

    low = lax.broadcasted_iota(jnp.int32, (C, 128), 1) < 64

    def dscores(grp):
        @pl.loop(0, 4)
        def _(n):
            dqc = []
            for l in range(L):
                def row(ref):
                    return jnp.concatenate([ref[grp, pl.ds(l * 8 + 2 * n + k, 1), :] for k in range(2)], axis=1)

                a = pbuf[grp, l, n] * row(fac)
                ds = (a * (dpbuf[grp, l, n] - row(inn))).astype(BF16)
                cols = pl.ds(pl.multiple_of(n * 256, 256), 256)
                dsb[l, :, cols] = ds
                alb[l, :, cols] = a.astype(BF16)
                dqc.append(jnp.dot(kt[l], ds, preferred_element_type=F32))
            for k in range(2):
                one, two = (v[:, 128 * k : 128 * k + 128] for v in dqc)
                even = jnp.where(low, one, pltpu.roll(two, 64, 1)).astype(BF16)
                odd = jnp.where(low, pltpu.roll(one, 64, 1), two).astype(BF16)
                for half in range(2):
                    rows = slice(128 * half, 128 * half + 128)
                    dqs[grp, half, n, 2 * k] = even[rows]
                    dqs[grp, half, n, 2 * k + 1] = odd[rows]

    def kv_grads(grp):
        for l in range(L):
            for k, left in enumerate((dsb, alb)):
                val = jnp.dot(left[l], qg[l, k, grp].reshape(N // 2, C), preferred_element_type=F32)
                if grp == 0:
                    kvacc[l, k] = val
                else:
                    grads[l, :, k * C : k * C + C] = (kvacc[l, k] + val).astype(BF16)

    def rs_first(grp):
        out = []
        for d in range(1, 4):
            out.append(put(dqs.at[grp, 0, (y + d) % 4], r1.at[grp, 0, d - 1], plane_device(0, 0, d)))
            out.append(put(dqs.at[grp, 1, :, (z + d) % 4], r1.at[grp, 1, d - 1], plane_device(1, 0, d)))
        return out

    def rs_second(grp, first):
        arrive(first)
        for half in range(2):
            own_part = dqs[grp, 0, y] if half == 0 else dqs[grp, 1, :, z]
            acc = own_part.astype(F32)
            for d in range(3):
                acc = acc + r1[grp, half, d].astype(F32)
            s1[grp, half] = acc.astype(BF16)
        out = []
        for d in range(1, 4):
            out.append(put(s1.at[grp, 0, (z + d) % 4], r2.at[grp, 0, d - 1], plane_device(0, 1, d)))
            out.append(put(s1.at[grp, 1, (y + d) % 4], r2.at[grp, 1, d - 1], plane_device(1, 1, d)))
        return out

    def rs_end(grp, second):
        arrive(second)
        for half in range(2):
            acc = (s1[grp, 0, z] if half == 0 else s1[grp, 1, y]).astype(F32)
            for d in range(3):
                acc = acc + r2[grp, half, d].astype(F32)
            dqt[grp, :, :, :, 128 * half : 128 * half + 128] = acc.T.reshape(2, 2, 32, 128).astype(BF16)
        if grp == 0:
            mine = load(dqt.at[0, :, core], ob.at[:, tgt, y, z])
            out = [put(dqt.at[0, :, 1 - core], ob.at[:, tgt, y, z], (inp, partner, mdl))]
            return out, mine
        out = []
        for r in range(2):
            c = (core + r) % 2
            out.append(put(dqt.at[1, :, c], ob.at[:, tgt, y, z], (inp, opp + c, mdl)))
        return out, None

    def oview(grp, ref=ob):
        first = xh * 2 if grp == 0 else opp
        return lambda half, yy, zz: ref.at[half, pl.ds(first, 2), yy, zz]

    def spread(grp):
        out = gather_phase(oview(grp), 1, oview(grp, dq_out))
        lines = ((0, slice(None), z), (1, y, slice(None)))
        return out, [load(oview(grp)(*line), oview(grp, dq_out)(*line)) for line in lines]

    def block(xx, cc):
        f = (xx // 2) * 4 + cc * 2 + xx % 2
        rows = pl.ds(pl.multiple_of(f * 512, 512), 512)
        acc = lax.dot_general(grads[0], w[0, rows, :], NT, preferred_element_type=F32)
        acc = acc + lax.dot_general(grads[1], w[1, rows, :], NT, preferred_element_type=F32)
        return acc.astype(BF16)

    def both(k, xx):
        eb[k, 0] = block(xx, 1 - core)
        cp = put(eb.at[k, 0], cr.at[k], at_x(x, 1 - core))
        eb[k, 1] = block(xx, core)
        return cp

    pl.semaphore_wait(barrier, len(friends))

    x_phase, x_whole, core_phase = [], [], []
    for r in range(2):
        there = opp + (core + r) % 2
        device = (inp, there, mdl)
        x_phase.append(put(g_hbm.at[there, 0, y, z], qg.at[0, 1, 1, y, z, core], device))
        x_phase.append(put(q_hbm.at[there, :, y, z], qg.at[:, 0, 1, y, z, core], device))
    for k, src in enumerate((q_hbm, g_hbm)):
        core_phase.append(put(src.at[partner], qg.at[:, k, 0, :, :, core], (inp, partner, mdl)))

    enc_load.wait()
    project(0)
    for r in range(2):
        there = opp + (core + r) % 2
        x_whole.append(put(g_hbm.at[there, 1], qg.at[1, 1, 1, :, :, core], (inp, there, mdl)))
    project(1)
    for cp in own:
        cp.wait()
    arrive(core_phase)
    scores(0, 0)
    scores(0, 1)
    sa = stats_out(0, 0)
    arrive(x_phase)
    q_a0 = gather_phase(qview(0), 0)
    q_a1 = gather_phase(qview(1), 0)
    stats_in(0, 0, sa)
    sa = stats_out(0, 1)
    arrive(q_a0)
    q_b0 = gather_phase(qview(0), 1)
    arrive(q_a1)
    q_b1 = gather_phase(qview(1), 1)
    stats_in(0, 1, sa)
    dscores(0)
    fa = rs_first(0)
    kv_grads(0)
    arrive(q_b0)
    scores(1, 0)
    arrive(q_b1)
    arrive(x_whole)
    scores(1, 1)
    sb = stats_out(1, 0)
    ea = rs_second(0, fa)
    stats_in(1, 0, sb)
    sb = stats_out(1, 1)
    xa, ma = rs_end(0, ea)
    stats_in(1, 1, sb)
    dscores(1)
    fb = rs_first(1)
    arrive(xa)
    ma.wait()
    aa = gather_phase(oview(0), 0)
    kv_grads(1)
    c_o = both(0, xo)
    c_p = both(1, xp)
    arrive([c_o])
    eb[0, 1] = eb[0, 1] + cr[0]
    ro = [
        put(eb.at[0, 1, pl.ds(0, 256)], rl.at[0], at_x(xp, core)),
        put(eb.at[0, 1, pl.ds(256, 256)], rl.at[1], at_x(xm, core)),
    ]
    c_m = both(2, xm)
    e2 = rs_second(1, fb)
    arrive(aa)
    ba, out_a = spread(0)
    arrive([c_p, c_m])
    eb[1, 1] = eb[1, 1] + cr[1]
    eb[2, 1] = eb[2, 1] + cr[2]
    n1 = [
        put(eb.at[1, 1, pl.ds(256, 256)], nb.at[0, pl.ds(256, 256)], at_x(xp, core)),
        put(eb.at[2, 1, pl.ds(0, 256)], nb.at[1, pl.ds(0, 256)], at_x(xm, core)),
    ]
    xb, _ = rs_end(1, e2)
    c_s = both(3, x)
    arrive(ro)
    eb[1, 1, 0:256] = eb[1, 1, 0:256] + rl[0]
    eb[2, 1, 256:512] = eb[2, 1, 256:512] + rl[1]
    n2 = [
        put(eb.at[1, 1, pl.ds(0, 256)], nb.at[0, pl.ds(0, 256)], at_x(xp, core)),
        put(eb.at[2, 1, pl.ds(256, 256)], nb.at[1, pl.ds(256, 256)], at_x(xm, core)),
    ]
    arrive(xb)
    ab = gather_phase(oview(1), 0)
    arrive([c_s])
    arrive(ab)
    bb, out_b = spread(1)
    arrive(n1)
    arrive(n2)
    enc_out[...] = (
        eb[3, 1].astype(F32) + cr[3].astype(F32) + nb[0].astype(F32) + nb[1].astype(F32)
    ).astype(BF16)
    arrive(ba)
    arrive(bb)
    for cp in sent:
        cp.wait_send()
    for cp in out_a + out_b:
        cp.wait()


def body(encoder, key_weight, value_weight, queries, grad_out):
    kw = key_weight.reshape(L, D, C)
    vw = value_weight.reshape(L, D, C)
    q = jnp.transpose(queries, (2, 0, 1, 3)).reshape(4, L, 4, 4, 32, C)
    g = jnp.transpose(grad_out, (2, 0, 1, 3)).reshape(4, L, 4, 4, 32, C)
    anywhere = pl.BlockSpec(memory_space=pl.ANY)
    dq, de = pl.pallas_call(
        kernel,
        out_shape=(
            jax.ShapeDtypeStruct((L, 4, 4, 4, 32, C), BF16),
            jax.ShapeDtypeStruct((E, 512), BF16),
        ),
        in_specs=[anywhere] * 5,
        out_specs=(anywhere, pl.BlockSpec(memory_space=pltpu.VMEM)),
        scratch_shapes=[
            pltpu.VMEM((E, D), BF16),
            pltpu.VMEM((L, D, 2 * C), BF16),
            pltpu.VMEM((L, 2, 2, 4, 4, 2, 32, C), BF16),
            pltpu.VMEM((L, E, 2 * C), BF16),
            pltpu.VMEM((L, C, E), BF16),
            pltpu.VMEM((2, L, 4, E, 256), F32),
            pltpu.VMEM((2, L, 4, E, 256), F32),
            pltpu.VMEM((L, E, N // 2), BF16),
            pltpu.VMEM((L, E, N // 2), BF16),
            pltpu.VMEM((2, 3, 16, 128), F32),
            pltpu.VMEM((2, 2, 3, 3, 16, 128), F32),
            pltpu.VMEM((2, 3, 16, 128), F32),
            pltpu.VMEM((2, 16, 128), F32),
            pltpu.VMEM((2, 16, 128), F32),
            pltpu.VMEM((2, 2, 4, 4, 128, 128), BF16),
            pltpu.VMEM((2, 2, 3, 4, 128, 128), BF16),
            pltpu.VMEM((2, 2, 4, 128, 128), BF16),
            pltpu.VMEM((2, 2, 3, 128, 128), BF16),
            pltpu.VMEM((2, L, 2, 32, C), BF16),
            pltpu.VMEM((L, 4, 4, 4, 32, C), BF16),
            pltpu.VMEM((L, 2, E, C), F32),
            pltpu.VMEM((L, E, 2 * C), BF16),
            pltpu.VMEM((4, 2, E, 512), BF16),
            pltpu.VMEM((4, E, 512), BF16),
            pltpu.VMEM((2, 256, 512), BF16),
            pltpu.VMEM((2, E, 512), BF16),
            pltpu.SemaphoreType.DMA((NSEM,)),
            pltpu.SemaphoreType.DMA((NSEM,)),
            pltpu.SemaphoreType.DMA((16,)),
        ],
        compiler_params=pltpu.CompilerParams(
            collective_id=0, has_side_effects=True, vmem_limit_bytes=60 * 2**20
        ),
        cost_estimate=pl.CostEstimate(flops=14_000_000_000, bytes_accessed=20_000_000, transcendentals=2_000_000),
    )(encoder, kw, vw, q, g)
    dq = jnp.transpose(dq.reshape(L, 4, 512, C), (0, 2, 1, 3))
    return dq, de


def solution(mesh):
    placed = (
        P("inp", None),
        P(None, None, "mdl", "tgt", None),
        P(None, None, "mdl", "tgt", None),
        P(None, "tgt", "mdl", None),
        P(None, "tgt", "mdl", None),
    )
    return jax.shard_map(
        body,
        mesh=mesh,
        in_specs=placed,
        out_specs=(P(None, "tgt", "mdl", None), P("inp", ("tgt", "mdl"))),
        check_vma=False,
    )
```

```python
import functools

import jax
import jax.numpy as jnp
from jax import lax
from jax.experimental import pallas as pl
from jax.experimental.pallas import tpu as pltpu
from jax.sharding import PartitionSpec as P

MESH = pl.DeviceIdType.MESH
F32 = jnp.float32
BF16 = jnp.bfloat16
NT = (((1,), (1,)), ((), ()))

E = 512
D = 4096
C = 256
L = 2
N = 2048
NSEM = 108


def kernel(
    enc_hbm, kw_hbm, vw_hbm, q_hbm, g_hbm,
    dq_out, enc_out,
    enc, w, qg, kv, kt, pbuf, dpbuf, dsb, alb,
    stat_s, stat_r, stat_c, fac, inn,
    dqs, r1, s1, r2, dqt, ob,
    kvacc, grads, eb, cr, rl, nb,
    send_sems, recv_sems, local_sems,
):
    inp = lax.axis_index("inp")
    tgt = lax.axis_index("tgt")
    mdl = lax.axis_index("mdl")
    y, z = inp // 4, inp % 4
    xh, core = tgt // 2, tgt % 2
    x = xh * 2 + mdl
    opp = (1 - xh) * 2
    partner = xh * 2 + (1 - core)
    xp, xm, xo = (x + 1) % 4, (x + 3) % 4, (x + 2) % 4

    def at_yz(yy, zz):
        return (yy * 4 + zz, tgt, mdl)

    def at_x(xx, cc):
        return (inp, (xx // 2) * 2 + cc, xx % 2)

    counter = [0]
    sent = []

    def put(src, dst, device):
        k = counter[0]
        counter[0] += 1
        cp = pltpu.make_async_remote_copy(
            src_ref=src, dst_ref=dst, send_sem=send_sems.at[k], recv_sem=recv_sems.at[k],
            device_id=device, device_id_type=MESH,
        )
        cp.start()
        sent.append(cp)
        return cp

    local_counter = [0]

    def load(src, dst):
        k = local_counter[0]
        local_counter[0] += 1
        cp = pltpu.make_async_copy(src, dst, local_sems.at[k])
        cp.start()
        return cp

    def arrive(cps):
        for cp in cps:
            cp.wait_recv()

    barrier = pltpu.get_barrier_semaphore()
    friends = [at_yz((y + d) % 4, z) for d in range(1, 4)] + [at_yz(y, (z + d) % 4) for d in range(1, 4)]
    friends += [(inp, partner, mdl), (inp, opp, mdl), (inp, opp + 1, mdl), at_x(xp, core), at_x(xm, core)]
    for friend in friends:
        pl.semaphore_signal(barrier, inc=1, device_id=friend, device_id_type=MESH)

    enc_load = load(enc_hbm, enc)
    w_loads = []
    for l in range(L):
        w_loads.append(
            (load(kw_hbm.at[l], w.at[l, :, pl.ds(0, C)]), load(vw_hbm.at[l], w.at[l, :, pl.ds(C, C)]))
        )
        if l == 0:
            own = [load(src.at[tgt], qg.at[:, k, 0, :, :, core]) for k, src in enumerate((q_hbm, g_hbm))]

    def plane_device(half, phase, d):
        if (half == 0) == (phase == 0):
            return at_yz((y + d) % 4, z)
        return at_yz(y, (z + d) % 4)

    def gather_phase(view, phase, to=None):
        to = to or view
        out = []
        for d in range(1, 4):
            for half in range(2):
                if phase == 0:
                    place = (half, y, z)
                elif half == 0:
                    place = (half, slice(None), z)
                else:
                    place = (half, y, slice(None))
                out.append(put(view(*place), to(*place), plane_device(half, phase, d)))
        return out

    def qview(l):
        return lambda half, yy, zz: qg.at[l, half, 1, yy, zz]

    def project(l):
        for cp in w_loads[l]:
            cp.wait()
        kv[l] = jnp.dot(enc[...], w[l], preferred_element_type=F32).astype(BF16)
        kt[l] = kv[l, :, 0:C].astype(F32).T.astype(BF16)

    def scores(grp, l):
        @pl.loop(0, 4)
        def _(n):
            qc = qg[l, 0, grp, n].reshape(256, C)
            gc = qg[l, 1, grp, n].reshape(256, C)
            st = lax.dot_general(kv[l, :, 0:C], qc, NT, preferred_element_type=F32)
            dp = lax.dot_general(kv[l, :, C : 2 * C], gc, NT, preferred_element_type=F32)
            peak = jnp.max(st, axis=0, keepdims=True)
            p = jnp.exp(st - peak)
            pbuf[grp, l, n] = p
            dpbuf[grp, l, n] = dp
            total = jnp.sum(p, axis=0, keepdims=True)
            inner = jnp.sum(p * dp, axis=0, keepdims=True)
            for k in range(2):
                cols = slice(128 * k, 128 * k + 128)
                row = pl.ds(l * 8 + 2 * n + k, 1)
                stat_s[grp, 0, row, :] = peak[:, cols]
                stat_s[grp, 1, row, :] = total[:, cols]
                stat_s[grp, 2, row, :] = inner[:, cols]

    def stats_out(grp, phase):
        src = (stat_s if phase == 0 else stat_c).at[grp]
        return [put(src, stat_r.at[grp, phase, d - 1], plane_device(0, phase, d)) for d in range(1, 4)]

    def stats_in(grp, phase, cps):
        arrive(cps)
        src = stat_s if phase == 0 else stat_c
        terms = [(src[grp, 0], src[grp, 1], src[grp, 2])]
        for d in range(3):
            terms.append((stat_r[grp, phase, d, 0], stat_r[grp, phase, d, 1], stat_r[grp, phase, d, 2]))
        peak = jnp.maximum(jnp.maximum(terms[0][0], terms[1][0]), jnp.maximum(terms[2][0], terms[3][0]))
        scale = [jnp.exp(t[0] - peak) for t in terms]
        total = sum(t[1] * f for t, f in zip(terms, scale))
        inner = sum(t[2] * f for t, f in zip(terms, scale))
        if phase == 0:
            stat_c[grp, 0] = peak
            stat_c[grp, 1] = total
            stat_c[grp, 2] = inner
        else:
            fac[grp] = jnp.exp(stat_s[grp, 0] - peak) / total
            inn[grp] = inner / total

    low = lax.broadcasted_iota(jnp.int32, (C, 128), 1) < 64

    def dscores(grp):
        @pl.loop(0, 4)
        def _(n):
            dqc = []
            for l in range(L):
                def row(ref):
                    return jnp.concatenate([ref[grp, pl.ds(l * 8 + 2 * n + k, 1), :] for k in range(2)], axis=1)

                a = pbuf[grp, l, n] * row(fac)
                ds = (a * (dpbuf[grp, l, n] - row(inn))).astype(BF16)
                cols = pl.ds(pl.multiple_of(n * 256, 256), 256)
                dsb[l, :, cols] = ds
                alb[l, :, cols] = a.astype(BF16)
                dqc.append(jnp.dot(kt[l], ds, preferred_element_type=F32))
            for k in range(2):
                one, two = (v[:, 128 * k : 128 * k + 128] for v in dqc)
                even = jnp.where(low, one, pltpu.roll(two, 64, 1)).astype(BF16)
                odd = jnp.where(low, pltpu.roll(one, 64, 1), two).astype(BF16)
                for half in range(2):
                    rows = slice(128 * half, 128 * half + 128)
                    dqs[grp, half, n, 2 * k] = even[rows]
                    dqs[grp, half, n, 2 * k + 1] = odd[rows]

    def kv_grads(grp):
        for l in range(L):
            for k, left in enumerate((dsb, alb)):
                val = jnp.dot(left[l], qg[l, k, grp].reshape(N // 2, C), preferred_element_type=F32)
                if grp == 0:
                    kvacc[l, k] = val
                else:
                    grads[l, :, k * C : k * C + C] = (kvacc[l, k] + val).astype(BF16)

    def rs_first(grp):
        out = []
        for d in range(1, 4):
            out.append(put(dqs.at[grp, 0, (y + d) % 4], r1.at[grp, 0, d - 1], plane_device(0, 0, d)))
            out.append(put(dqs.at[grp, 1, :, (z + d) % 4], r1.at[grp, 1, d - 1], plane_device(1, 0, d)))
        return out

    def rs_second(grp, first):
        arrive(first)
        for half in range(2):
            own_part = dqs[grp, 0, y] if half == 0 else dqs[grp, 1, :, z]
            acc = own_part.astype(F32)
            for d in range(3):
                acc = acc + r1[grp, half, d].astype(F32)
            s1[grp, half] = acc.astype(BF16)
        out = []
        for d in range(1, 4):
            out.append(put(s1.at[grp, 0, (z + d) % 4], r2.at[grp, 0, d - 1], plane_device(0, 1, d)))
            out.append(put(s1.at[grp, 1, (y + d) % 4], r2.at[grp, 1, d - 1], plane_device(1, 1, d)))
        return out

    def rs_end(grp, second):
        arrive(second)
        for half in range(2):
            acc = (s1[grp, 0, z] if half == 0 else s1[grp, 1, y]).astype(F32)
            for d in range(3):
                acc = acc + r2[grp, half, d].astype(F32)
            dqt[grp, :, :, :, 128 * half : 128 * half + 128] = acc.T.reshape(2, 2, 32, 128).astype(BF16)
        if grp == 0:
            mine = load(dqt.at[0, :, core], ob.at[:, tgt, y, z])
            out = [put(dqt.at[0, :, 1 - core], ob.at[:, tgt, y, z], (inp, partner, mdl))]
            return out, mine
        out = []
        for r in range(2):
            c = (core + r) % 2
            out.append(put(dqt.at[1, :, c], ob.at[:, tgt, y, z], (inp, opp + c, mdl)))
        return out, None

    def oview(grp, ref=ob):
        first = xh * 2 if grp == 0 else opp
        return lambda half, yy, zz: ref.at[half, pl.ds(first, 2), yy, zz]

    def spread(grp):
        out = gather_phase(oview(grp), 1, oview(grp, dq_out))
        lines = ((0, slice(None), z), (1, y, slice(None)))
        return out, [load(oview(grp)(*line), oview(grp, dq_out)(*line)) for line in lines]

    def block(xx, cc):
        f = (xx // 2) * 4 + cc * 2 + xx % 2
        rows = pl.ds(pl.multiple_of(f * 512, 512), 512)
        acc = lax.dot_general(grads[0], w[0, rows, :], NT, preferred_element_type=F32)
        acc = acc + lax.dot_general(grads[1], w[1, rows, :], NT, preferred_element_type=F32)
        return acc.astype(BF16)

    def both(k, xx):
        eb[k, 0] = block(xx, 1 - core)
        cp = put(eb.at[k, 0], cr.at[k], at_x(x, 1 - core))
        eb[k, 1] = block(xx, core)
        return cp

    pl.semaphore_wait(barrier, len(friends))

    x_phase, x_whole, core_phase = [], [], []
    for r in range(2):
        there = opp + (core + r) % 2
        device = (inp, there, mdl)
        x_phase.append(put(g_hbm.at[there, 0, y, z], qg.at[0, 1, 1, y, z, core], device))
        x_phase.append(put(q_hbm.at[there, 0, y, z], qg.at[0, 0, 1, y, z, core], device))
    for k, src in enumerate((q_hbm, g_hbm)):
        core_phase.append(put(src.at[partner], qg.at[:, k, 0, :, :, core], (inp, partner, mdl)))

    enc_load.wait()
    project(0)
    for r in range(2):
        there = opp + (core + r) % 2
        for k, src in enumerate((q_hbm, g_hbm)):
            x_whole.append(put(src.at[there, 1], qg.at[1, k, 1, :, :, core], (inp, there, mdl)))
    project(1)
    for cp in own:
        cp.wait()
    arrive(core_phase)
    scores(0, 0)
    scores(0, 1)
    sa = stats_out(0, 0)
    arrive(x_phase)
    q_a0 = gather_phase(qview(0), 0)
    stats_in(0, 0, sa)
    sa = stats_out(0, 1)
    arrive(q_a0)
    q_b0 = gather_phase(qview(0), 1)
    stats_in(0, 1, sa)
    dscores(0)
    fa = rs_first(0)
    kv_grads(0)
    arrive(q_b0)
    scores(1, 0)
    arrive(x_whole)
    scores(1, 1)
    sb = stats_out(1, 0)
    ea = rs_second(0, fa)
    stats_in(1, 0, sb)
    sb = stats_out(1, 1)
    xa, ma = rs_end(0, ea)
    stats_in(1, 1, sb)
    dscores(1)
    fb = rs_first(1)
    arrive(xa)
    ma.wait()
    aa = gather_phase(oview(0), 0)
    kv_grads(1)
    c_o = both(0, xo)
    c_p = both(1, xp)
    arrive([c_o])
    eb[0, 1] = eb[0, 1] + cr[0]
    ro = [
        put(eb.at[0, 1, pl.ds(0, 256)], rl.at[0], at_x(xp, core)),
        put(eb.at[0, 1, pl.ds(256, 256)], rl.at[1], at_x(xm, core)),
    ]
    c_m = both(2, xm)
    e2 = rs_second(1, fb)
    arrive(aa)
    ba, out_a = spread(0)
    arrive([c_p, c_m])
    eb[1, 1] = eb[1, 1] + cr[1]
    eb[2, 1] = eb[2, 1] + cr[2]
    n1 = [
        put(eb.at[1, 1, pl.ds(256, 256)], nb.at[0, pl.ds(256, 256)], at_x(xp, core)),
        put(eb.at[2, 1, pl.ds(0, 256)], nb.at[1, pl.ds(0, 256)], at_x(xm, core)),
    ]
    xb, _ = rs_end(1, e2)
    c_s = both(3, x)
    arrive(ro)
    eb[1, 1, 0:256] = eb[1, 1, 0:256] + rl[0]
    eb[2, 1, 256:512] = eb[2, 1, 256:512] + rl[1]
    n2 = [
        put(eb.at[1, 1, pl.ds(0, 256)], nb.at[0, pl.ds(0, 256)], at_x(xp, core)),
        put(eb.at[2, 1, pl.ds(256, 256)], nb.at[1, pl.ds(256, 256)], at_x(xm, core)),
    ]
    arrive(xb)
    ab = gather_phase(oview(1), 0)
    arrive([c_s])
    arrive(ab)
    bb, out_b = spread(1)
    arrive(n1)
    arrive(n2)
    enc_out[...] = (
        eb[3, 1].astype(F32) + cr[3].astype(F32) + nb[0].astype(F32) + nb[1].astype(F32)
    ).astype(BF16)
    arrive(ba)
    arrive(bb)
    for cp in sent:
        cp.wait_send()
    for cp in out_a + out_b:
        cp.wait()


def body(encoder, key_weight, value_weight, queries, grad_out):
    kw = key_weight.reshape(L, D, C)
    vw = value_weight.reshape(L, D, C)
    q = jnp.transpose(queries, (2, 0, 1, 3)).reshape(4, L, 4, 4, 32, C)
    g = jnp.transpose(grad_out, (2, 0, 1, 3)).reshape(4, L, 4, 4, 32, C)
    anywhere = pl.BlockSpec(memory_space=pl.ANY)
    dq, de = pl.pallas_call(
        kernel,
        out_shape=(
            jax.ShapeDtypeStruct((L, 4, 4, 4, 32, C), BF16),
            jax.ShapeDtypeStruct((E, 512), BF16),
        ),
        in_specs=[anywhere] * 5,
        out_specs=(anywhere, pl.BlockSpec(memory_space=pltpu.VMEM)),
        scratch_shapes=[
            pltpu.VMEM((E, D), BF16),
            pltpu.VMEM((L, D, 2 * C), BF16),
            pltpu.VMEM((L, 2, 2, 4, 4, 2, 32, C), BF16),
            pltpu.VMEM((L, E, 2 * C), BF16),
            pltpu.VMEM((L, C, E), BF16),
            pltpu.VMEM((2, L, 4, E, 256), F32),
            pltpu.VMEM((2, L, 4, E, 256), F32),
            pltpu.VMEM((L, E, N // 2), BF16),
            pltpu.VMEM((L, E, N // 2), BF16),
            pltpu.VMEM((2, 3, 16, 128), F32),
            pltpu.VMEM((2, 2, 3, 3, 16, 128), F32),
            pltpu.VMEM((2, 3, 16, 128), F32),
            pltpu.VMEM((2, 16, 128), F32),
            pltpu.VMEM((2, 16, 128), F32),
            pltpu.VMEM((2, 2, 4, 4, 128, 128), BF16),
            pltpu.VMEM((2, 2, 3, 4, 128, 128), BF16),
            pltpu.VMEM((2, 2, 4, 128, 128), BF16),
            pltpu.VMEM((2, 2, 3, 128, 128), BF16),
            pltpu.VMEM((2, L, 2, 32, C), BF16),
            pltpu.VMEM((L, 4, 4, 4, 32, C), BF16),
            pltpu.VMEM((L, 2, E, C), F32),
            pltpu.VMEM((L, E, 2 * C), BF16),
            pltpu.VMEM((4, 2, E, 512), BF16),
            pltpu.VMEM((4, E, 512), BF16),
            pltpu.VMEM((2, 256, 512), BF16),
            pltpu.VMEM((2, E, 512), BF16),
            pltpu.SemaphoreType.DMA((NSEM,)),
            pltpu.SemaphoreType.DMA((NSEM,)),
            pltpu.SemaphoreType.DMA((16,)),
        ],
        compiler_params=pltpu.CompilerParams(
            collective_id=0, has_side_effects=True, vmem_limit_bytes=60 * 2**20
        ),
        cost_estimate=pl.CostEstimate(flops=14_000_000_000, bytes_accessed=20_000_000, transcendentals=2_000_000),
    )(encoder, kw, vw, q, g)
    dq = jnp.transpose(dq.reshape(L, 4, 512, C), (0, 2, 1, 3))
    return dq, de


def solution(mesh):
    placed = (
        P("inp", None),
        P(None, None, "mdl", "tgt", None),
        P(None, None, "mdl", "tgt", None),
        P(None, "tgt", "mdl", None),
        P(None, "tgt", "mdl", None),
    )
    return jax.shard_map(
        body,
        mesh=mesh,
        in_specs=placed,
        out_specs=(P(None, "tgt", "mdl", None), P("inp", ("tgt", "mdl"))),
        check_vma=False,
    )
```

```python
import functools

import jax
import jax.numpy as jnp
from jax import lax
from jax.experimental import pallas as pl
from jax.experimental.pallas import tpu as pltpu
from jax.sharding import PartitionSpec as P

MESH = pl.DeviceIdType.MESH
F32 = jnp.float32
BF16 = jnp.bfloat16
NT = (((1,), (1,)), ((), ()))

E = 512
D = 4096
C = 256
L = 2
N = 2048
NSEM = 108


def kernel(
    enc_hbm, kw_hbm, vw_hbm, q_hbm, g_hbm,
    dq_out, enc_out,
    enc, w, qg, kv, kt, pbuf, dpbuf, dsb, alb,
    stat_s, stat_r, stat_c, fac, inn,
    dqs, r1, s1, r2, dqt, ob,
    kvacc, grads, eb, cr, rl, nb,
    send_sems, recv_sems, local_sems,
):
    inp = lax.axis_index("inp")
    tgt = lax.axis_index("tgt")
    mdl = lax.axis_index("mdl")
    y, z = inp // 4, inp % 4
    xh, core = tgt // 2, tgt % 2
    x = xh * 2 + mdl
    opp = (1 - xh) * 2
    partner = xh * 2 + (1 - core)
    xp, xm, xo = (x + 1) % 4, (x + 3) % 4, (x + 2) % 4

    def at_yz(yy, zz):
        return (yy * 4 + zz, tgt, mdl)

    def at_x(xx, cc):
        return (inp, (xx // 2) * 2 + cc, xx % 2)

    counter = [0]
    sent = []

    def put(src, dst, device):
        k = counter[0]
        counter[0] += 1
        cp = pltpu.make_async_remote_copy(
            src_ref=src, dst_ref=dst, send_sem=send_sems.at[k], recv_sem=recv_sems.at[k],
            device_id=device, device_id_type=MESH,
        )
        cp.start()
        sent.append(cp)
        return cp

    local_counter = [0]

    def load(src, dst):
        k = local_counter[0]
        local_counter[0] += 1
        cp = pltpu.make_async_copy(src, dst, local_sems.at[k])
        cp.start()
        return cp

    def arrive(cps):
        for cp in cps:
            cp.wait_recv()

    barrier = pltpu.get_barrier_semaphore()
    friends = [at_yz((y + d) % 4, z) for d in range(1, 4)] + [at_yz(y, (z + d) % 4) for d in range(1, 4)]
    friends += [(inp, partner, mdl), (inp, opp, mdl), (inp, opp + 1, mdl), at_x(xp, core), at_x(xm, core)]
    for friend in friends:
        pl.semaphore_signal(barrier, inc=1, device_id=friend, device_id_type=MESH)

    enc_load = load(enc_hbm, enc)
    w_loads = []
    for l in range(L):
        w_loads.append(
            (load(kw_hbm.at[l], w.at[l, :, pl.ds(0, C)]), load(vw_hbm.at[l], w.at[l, :, pl.ds(C, C)]))
        )
        if l == 0:
            own = [load(src.at[tgt], qg.at[:, k, 0, :, :, core]) for k, src in enumerate((q_hbm, g_hbm))]

    def plane_device(half, phase, d):
        if (half == 0) == (phase == 0):
            return at_yz((y + d) % 4, z)
        return at_yz(y, (z + d) % 4)

    def gather_phase(view, phase, to=None):
        to = to or view
        out = []
        for d in range(1, 4):
            for half in range(2):
                if phase == 0:
                    place = (half, y, z)
                elif half == 0:
                    place = (half, slice(None), z)
                else:
                    place = (half, y, slice(None))
                out.append(put(view(*place), to(*place), plane_device(half, phase, d)))
        return out

    def qview(l):
        return lambda half, yy, zz: qg.at[l, half, 1, yy, zz]

    def project(l):
        for cp in w_loads[l]:
            cp.wait()
        kv[l] = jnp.dot(enc[...], w[l], preferred_element_type=F32).astype(BF16)
        kt[l] = kv[l, :, 0:C].astype(F32).T.astype(BF16)

    def scores(grp, l):
        @pl.loop(0, 4)
        def _(n):
            qc = qg[l, 0, grp, n].reshape(256, C)
            gc = qg[l, 1, grp, n].reshape(256, C)
            st = lax.dot_general(kv[l, :, 0:C], qc, NT, preferred_element_type=F32)
            dp = lax.dot_general(kv[l, :, C : 2 * C], gc, NT, preferred_element_type=F32)
            peak = jnp.max(st, axis=0, keepdims=True)
            p = jnp.exp(st - peak)
            pbuf[grp, l, n] = p
            dpbuf[grp, l, n] = dp
            total = jnp.sum(p, axis=0, keepdims=True)
            inner = jnp.sum(p * dp, axis=0, keepdims=True)
            for k in range(2):
                cols = slice(128 * k, 128 * k + 128)
                row = pl.ds(l * 8 + 2 * n + k, 1)
                stat_s[grp, 0, row, :] = peak[:, cols]
                stat_s[grp, 1, row, :] = total[:, cols]
                stat_s[grp, 2, row, :] = inner[:, cols]

    def stats_out(grp, phase):
        src = (stat_s if phase == 0 else stat_c).at[grp]
        return [put(src, stat_r.at[grp, phase, d - 1], plane_device(0, phase, d)) for d in range(1, 4)]

    def stats_in(grp, phase, cps):
        arrive(cps)
        src = stat_s if phase == 0 else stat_c
        terms = [(src[grp, 0], src[grp, 1], src[grp, 2])]
        for d in range(3):
            terms.append((stat_r[grp, phase, d, 0], stat_r[grp, phase, d, 1], stat_r[grp, phase, d, 2]))
        peak = jnp.maximum(jnp.maximum(terms[0][0], terms[1][0]), jnp.maximum(terms[2][0], terms[3][0]))
        scale = [jnp.exp(t[0] - peak) for t in terms]
        total = sum(t[1] * f for t, f in zip(terms, scale))
        inner = sum(t[2] * f for t, f in zip(terms, scale))
        if phase == 0:
            stat_c[grp, 0] = peak
            stat_c[grp, 1] = total
            stat_c[grp, 2] = inner
        else:
            fac[grp] = jnp.exp(stat_s[grp, 0] - peak) / total
            inn[grp] = inner / total

    low = lax.broadcasted_iota(jnp.int32, (C, 128), 1) < 64

    def dscores(grp):
        @pl.loop(0, 4)
        def _(n):
            dqc = []
            for l in range(L):
                def row(ref):
                    return jnp.concatenate([ref[grp, pl.ds(l * 8 + 2 * n + k, 1), :] for k in range(2)], axis=1)

                a = pbuf[grp, l, n] * row(fac)
                ds = (a * (dpbuf[grp, l, n] - row(inn))).astype(BF16)
                cols = pl.ds(pl.multiple_of(n * 256, 256), 256)
                dsb[l, :, cols] = ds
                alb[l, :, cols] = a.astype(BF16)
                dqc.append(jnp.dot(kt[l], ds, preferred_element_type=F32))
            for k in range(2):
                one, two = (v[:, 128 * k : 128 * k + 128] for v in dqc)
                even = jnp.where(low, one, pltpu.roll(two, 64, 1)).astype(BF16)
                odd = jnp.where(low, pltpu.roll(one, 64, 1), two).astype(BF16)
                for half in range(2):
                    rows = slice(128 * half, 128 * half + 128)
                    dqs[grp, half, n, 2 * k] = even[rows]
                    dqs[grp, half, n, 2 * k + 1] = odd[rows]

    def kv_grads(grp):
        for l in range(L):
            for k, left in enumerate((dsb, alb)):
                val = jnp.dot(left[l], qg[l, k, grp].reshape(N // 2, C), preferred_element_type=F32)
                if grp == 0:
                    kvacc[l, k] = val
                else:
                    grads[l, :, k * C : k * C + C] = (kvacc[l, k] + val).astype(BF16)

    def rs_first(grp):
        out = []
        for d in range(1, 4):
            out.append(put(dqs.at[grp, 0, (y + d) % 4], r1.at[grp, 0, d - 1], plane_device(0, 0, d)))
            out.append(put(dqs.at[grp, 1, :, (z + d) % 4], r1.at[grp, 1, d - 1], plane_device(1, 0, d)))
        return out

    def rs_second(grp, first):
        arrive(first)
        for half in range(2):
            own_part = dqs[grp, 0, y] if half == 0 else dqs[grp, 1, :, z]
            acc = own_part.astype(F32)
            for d in range(3):
                acc = acc + r1[grp, half, d].astype(F32)
            s1[grp, half] = acc.astype(BF16)
        out = []
        for d in range(1, 4):
            out.append(put(s1.at[grp, 0, (z + d) % 4], r2.at[grp, 0, d - 1], plane_device(0, 1, d)))
            out.append(put(s1.at[grp, 1, (y + d) % 4], r2.at[grp, 1, d - 1], plane_device(1, 1, d)))
        return out

    def rs_end(grp, second):
        arrive(second)
        for half in range(2):
            acc = (s1[grp, 0, z] if half == 0 else s1[grp, 1, y]).astype(F32)
            for d in range(3):
                acc = acc + r2[grp, half, d].astype(F32)
            dqt[grp, :, :, :, 128 * half : 128 * half + 128] = acc.T.reshape(2, 2, 32, 128).astype(BF16)
        if grp == 0:
            mine = load(dqt.at[0, :, core], ob.at[:, tgt, y, z])
            out = [put(dqt.at[0, :, 1 - core], ob.at[:, tgt, y, z], (inp, partner, mdl))]
            return out, mine
        out = []
        for r in range(2):
            c = (core + r) % 2
            out.append(put(dqt.at[1, :, c], ob.at[:, tgt, y, z], (inp, opp + c, mdl)))
        return out, None

    def oview(grp, ref=ob):
        first = xh * 2 if grp == 0 else opp
        return lambda half, yy, zz: ref.at[half, pl.ds(first, 2), yy, zz]

    def spread(grp):
        out = gather_phase(oview(grp), 1, oview(grp, dq_out))
        lines = ((0, slice(None), z), (1, y, slice(None)))
        return out, [load(oview(grp)(*line), oview(grp, dq_out)(*line)) for line in lines]

    def block(xx, cc):
        f = (xx // 2) * 4 + cc * 2 + xx % 2
        rows = pl.ds(pl.multiple_of(f * 512, 512), 512)
        acc = lax.dot_general(grads[0], w[0, rows, :], NT, preferred_element_type=F32)
        acc = acc + lax.dot_general(grads[1], w[1, rows, :], NT, preferred_element_type=F32)
        return acc.astype(BF16)

    def both(k, xx):
        eb[k, 0] = block(xx, 1 - core)
        cp = put(eb.at[k, 0], cr.at[k], at_x(x, 1 - core))
        eb[k, 1] = block(xx, core)
        return cp

    pl.semaphore_wait(barrier, len(friends))

    x_phase, x_whole, core_phase = [], [], []
    for r in range(2):
        there = opp + (core + r) % 2
        device = (inp, there, mdl)
        x_phase.append(put(g_hbm.at[there, 0, y, z], qg.at[0, 1, 1, y, z, core], device))
        x_phase.append(put(q_hbm.at[there, 0, y, z], qg.at[0, 0, 1, y, z, core], device))
    for k, src in enumerate((q_hbm, g_hbm)):
        core_phase.append(put(src.at[partner], qg.at[:, k, 0, :, :, core], (inp, partner, mdl)))
    for r in range(2):
        there = opp + (core + r) % 2
        for k, src in enumerate((q_hbm, g_hbm)):
            x_whole.append(put(src.at[there, 1], qg.at[1, k, 1, :, :, core], (inp, there, mdl)))

    enc_load.wait()
    project(0)
    project(1)
    for cp in own:
        cp.wait()
    arrive(core_phase)
    scores(0, 0)
    scores(0, 1)
    sa = stats_out(0, 0)
    arrive(x_phase)
    q_a0 = gather_phase(qview(0), 0)
    stats_in(0, 0, sa)
    sa = stats_out(0, 1)
    arrive(q_a0)
    q_b0 = gather_phase(qview(0), 1)
    stats_in(0, 1, sa)
    dscores(0)
    fa = rs_first(0)
    kv_grads(0)
    arrive(q_b0)
    scores(1, 0)
    arrive(x_whole)
    scores(1, 1)
    sb = stats_out(1, 0)
    ea = rs_second(0, fa)
    stats_in(1, 0, sb)
    sb = stats_out(1, 1)
    xa, ma = rs_end(0, ea)
    stats_in(1, 1, sb)
    dscores(1)
    fb = rs_first(1)
    arrive(xa)
    ma.wait()
    aa = gather_phase(oview(0), 0)
    kv_grads(1)
    c_o = both(0, xo)
    c_p = both(1, xp)
    arrive([c_o])
    eb[0, 1] = eb[0, 1] + cr[0]
    ro = [
        put(eb.at[0, 1, pl.ds(0, 256)], rl.at[0], at_x(xp, core)),
        put(eb.at[0, 1, pl.ds(256, 256)], rl.at[1], at_x(xm, core)),
    ]
    c_m = both(2, xm)
    e2 = rs_second(1, fb)
    arrive(aa)
    ba, out_a = spread(0)
    arrive([c_p, c_m])
    eb[1, 1] = eb[1, 1] + cr[1]
    eb[2, 1] = eb[2, 1] + cr[2]
    n1 = [
        put(eb.at[1, 1, pl.ds(256, 256)], nb.at[0, pl.ds(256, 256)], at_x(xp, core)),
        put(eb.at[2, 1, pl.ds(0, 256)], nb.at[1, pl.ds(0, 256)], at_x(xm, core)),
    ]
    xb, _ = rs_end(1, e2)
    c_s = both(3, x)
    arrive(ro)
    eb[1, 1, 0:256] = eb[1, 1, 0:256] + rl[0]
    eb[2, 1, 256:512] = eb[2, 1, 256:512] + rl[1]
    n2 = [
        put(eb.at[1, 1, pl.ds(0, 256)], nb.at[0, pl.ds(0, 256)], at_x(xp, core)),
        put(eb.at[2, 1, pl.ds(256, 256)], nb.at[1, pl.ds(256, 256)], at_x(xm, core)),
    ]
    arrive(xb)
    ab = gather_phase(oview(1), 0)
    arrive([c_s])
    arrive(ab)
    bb, out_b = spread(1)
    arrive(n1)
    arrive(n2)
    enc_out[...] = (
        eb[3, 1].astype(F32) + cr[3].astype(F32) + nb[0].astype(F32) + nb[1].astype(F32)
    ).astype(BF16)
    arrive(ba)
    arrive(bb)
    for cp in sent:
        cp.wait_send()
    for cp in out_a + out_b:
        cp.wait()


def body(encoder, key_weight, value_weight, queries, grad_out):
    kw = key_weight.reshape(L, D, C)
    vw = value_weight.reshape(L, D, C)
    q = jnp.transpose(queries, (2, 0, 1, 3)).reshape(4, L, 4, 4, 32, C)
    g = jnp.transpose(grad_out, (2, 0, 1, 3)).reshape(4, L, 4, 4, 32, C)
    anywhere = pl.BlockSpec(memory_space=pl.ANY)
    dq, de = pl.pallas_call(
        kernel,
        out_shape=(
            jax.ShapeDtypeStruct((L, 4, 4, 4, 32, C), BF16),
            jax.ShapeDtypeStruct((E, 512), BF16),
        ),
        in_specs=[anywhere] * 5,
        out_specs=(anywhere, pl.BlockSpec(memory_space=pltpu.VMEM)),
        scratch_shapes=[
            pltpu.VMEM((E, D), BF16),
            pltpu.VMEM((L, D, 2 * C), BF16),
            pltpu.VMEM((L, 2, 2, 4, 4, 2, 32, C), BF16),
            pltpu.VMEM((L, E, 2 * C), BF16),
            pltpu.VMEM((L, C, E), BF16),
            pltpu.VMEM((2, L, 4, E, 256), F32),
            pltpu.VMEM((2, L, 4, E, 256), F32),
            pltpu.VMEM((L, E, N // 2), BF16),
            pltpu.VMEM((L, E, N // 2), BF16),
            pltpu.VMEM((2, 3, 16, 128), F32),
            pltpu.VMEM((2, 2, 3, 3, 16, 128), F32),
            pltpu.VMEM((2, 3, 16, 128), F32),
            pltpu.VMEM((2, 16, 128), F32),
            pltpu.VMEM((2, 16, 128), F32),
            pltpu.VMEM((2, 2, 4, 4, 128, 128), BF16),
            pltpu.VMEM((2, 2, 3, 4, 128, 128), BF16),
            pltpu.VMEM((2, 2, 4, 128, 128), BF16),
            pltpu.VMEM((2, 2, 3, 128, 128), BF16),
            pltpu.VMEM((2, L, 2, 32, C), BF16),
            pltpu.VMEM((L, 4, 4, 4, 32, C), BF16),
            pltpu.VMEM((L, 2, E, C), F32),
            pltpu.VMEM((L, E, 2 * C), BF16),
            pltpu.VMEM((4, 2, E, 512), BF16),
            pltpu.VMEM((4, E, 512), BF16),
            pltpu.VMEM((2, 256, 512), BF16),
            pltpu.VMEM((2, E, 512), BF16),
            pltpu.SemaphoreType.DMA((NSEM,)),
            pltpu.SemaphoreType.DMA((NSEM,)),
            pltpu.SemaphoreType.DMA((16,)),
        ],
        compiler_params=pltpu.CompilerParams(
            collective_id=0, has_side_effects=True, vmem_limit_bytes=60 * 2**20
        ),
        cost_estimate=pl.CostEstimate(flops=14_000_000_000, bytes_accessed=20_000_000, transcendentals=2_000_000),
    )(encoder, kw, vw, q, g)
    dq = jnp.transpose(dq.reshape(L, 4, 512, C), (0, 2, 1, 3))
    return dq, de


def solution(mesh):
    placed = (
        P("inp", None),
        P(None, None, "mdl", "tgt", None),
        P(None, None, "mdl", "tgt", None),
        P(None, "tgt", "mdl", None),
        P(None, "tgt", "mdl", None),
    )
    return jax.shard_map(
        body,
        mesh=mesh,
        in_specs=placed,
        out_specs=(P(None, "tgt", "mdl", None), P("inp", ("tgt", "mdl"))),
        check_vma=False,
    )
```
